32 devices in a mesh: dp: 8 (over z, y), mp: 4 (over x, core).
Axes of the slice: x: 2, y: 2, z: 4, core: 2. Of those that a mesh axis runs over, the one named last changes fastest.
Arguments:
- tokens: bfloat16 [2048, 4096], P('dp', 'mp'), may hold values from -6 to 6
- norm_gain: float32 [4096], P('mp'), may hold values from 0.75 to 7.5
- w_gate: bfloat16 [4096, 6144], P('dp', 'mp'), may hold values from -0.09375 to 0.09375
- w_up: bfloat16 [4096, 6144], P('dp', 'mp'), may hold values from -0.09375 to 0.09375
- cotangent: bfloat16 [2048, 6144], P('dp', 'mp'), may hold values from -0.13183594 to 0.13183594
- decay_mask: int32 [2, 4096], replicated, may hold values 0 or 1
- radius: float32 [1], replicated, may hold values from 12.8 to 38.4
Outputs:
- grad_gain: float32 [4096], P('mp')
- grad_gate: float32 [4096, 6144], P('dp', 'mp')
- grad_up: float32 [4096, 6144], P('dp', 'mp')
The draws below stay inside these ranges and needn't reach their ends.
Inputs may be any that keep to these rules, and one draw needn't show every extreme that they name: `decay_mask`: 1 marks a row that is perturbed.
All inputs are finite; a program needn't handle non-finite values.
Results may differ from the reference program's by a relative error of at most 0.024.
Values may be sent and summed in bfloat16 or wider, within the bound.
A program may use at most 128 MiB of HBM per device.

```python
import math
import jax
import jax.numpy as jnp
from jax import lax

D = 4096
FF = 6144
TOK_DEV = 256
TOKENS = 2048
N_DP = 8
N_MP = 4


def draw_norm_gain(key, part):
    place = jnp.arange(D).astype(jnp.float32) / jnp.float32(max(D - 1, 1))
    base = jnp.exp(jnp.log(jnp.float32(3.0)) * place)
    noise = jnp.clip(1.0 + 0.1 * jax.random.normal(key, (D,), jnp.float32), 0.75, 1.25)
    return (base * noise).astype(jnp.float32)


def with_ends(array, stream_key, least, largest):
    index_at = [jax.random.randint(jax.random.fold_in(stream_key, axis), (), 0, length) for axis, length in enumerate(array.shape)]
    main_axis = array.shape.index(max(array.shape))
    beside = index_at[:main_axis] + [(index_at[main_axis] + 1) % array.shape[main_axis]] + index_at[main_axis + 1:]
    return array.at[tuple(index_at)].set(least).at[tuple(beside)].set(largest)


def levels(rng, dims, pieces, low, largest):
    level, own = 1.0, jax.random.fold_in(rng, 6)
    for axis_at, parts in pieces:
        heights = jnp.exp(jax.random.uniform(jax.random.fold_in(own, axis_at), (parts,), jnp.float32, low / len(pieces), largest / len(pieces)))
        level = level * jnp.repeat(heights, dims[axis_at] // parts).reshape([-1 if axis == axis_at else 1 for axis in range(len(dims))])
    return level


def centred(own_key, shape, width, limit, pieces=(), dtype=jnp.bfloat16):
    entries = width * jax.random.normal(own_key, shape, jnp.float32)
    if pieces:
        entries = entries * levels(own_key, shape, pieces, -0.22, 0.18)
    return jnp.clip(entries, -limit, limit).astype(dtype)


def setup_inputs(seed: int = 0) -> dict:
    key_of = jax.random.split(jax.random.key(seed), 8)
    return {
        "tokens": centred(key_of[0], (TOKENS, D), 1.0, 6.0, ((0, 8), (1, 4))),
        "norm_gain": draw_norm_gain(jax.random.fold_in(key_of[7], 71), 0),
        "w_gate": centred(key_of[2], (D, FF), D ** -0.5, 0.09375, ((0, 8), (1, 4))),
        "w_up": centred(key_of[3], (D, FF), D ** -0.5, 0.09375, ((0, 8), (1, 4))),
        "cotangent": centred(key_of[4], (TOKENS, FF), (TOKENS ** -0.5), 0.13183594, ((0, 8), (1, 4))),
        "decay_mask": with_ends((jax.random.randint(key_of[5], (2, D), 0, 2) < 1).astype(jnp.int32), jax.random.fold_in(key_of[5], 1), 0, 1),
        "radius": jnp.clip(jnp.exp(jax.random.uniform(key_of[6], (1,), jnp.float32, math.log(12.8), math.log(38.4))), 12.8, 38.4),
    }


def activation(value):
    return jax.nn.gelu(value, approximate=True)

def pass_grads(scaled, gain_vec, mat_gate, mat_up, cotangent):
    block = FF // N_MP
    normed = (scaled * gain_vec[None, :]).astype(jnp.bfloat16)
    pre_gate = jnp.dot(normed, mat_gate, preferred_element_type=jnp.float32)
    pre_up = jnp.dot(normed, mat_up, preferred_element_type=jnp.float32)
    activated, back_fn = jax.vjp(activation, pre_gate)
    upstream = cotangent.astype(jnp.float32)
    d_up = (upstream * activated).astype(jnp.bfloat16)
    d_gate = back_fn(upstream * pre_up)[0].astype(jnp.bfloat16)

    def feature_step(index, total):
        first = (index * block).astype(jnp.int32)
        gate_cols = lax.dynamic_slice_in_dim(d_gate, first, block, 1)
        up_cols = lax.dynamic_slice_in_dim(d_up, first, block, 1)
        gate_mat = lax.dynamic_slice_in_dim(mat_gate, first, block, 1)
        up_mat = lax.dynamic_slice_in_dim(mat_up, first, block, 1)
        term = lax.dot_general(gate_cols, gate_mat, (((1,), (1,)), ((), ())), preferred_element_type=jnp.float32)
        term = term + lax.dot_general(up_cols, up_mat, (((1,), (1,)), ((), ())), preferred_element_type=jnp.float32)
        term = lax.optimization_barrier(term.astype(jnp.bfloat16)).astype(jnp.float32)
        return total + term
    d_norm = lax.fori_loop(0, N_MP, feature_step, jnp.zeros((TOKENS, D), jnp.float32))
    d_gain = lax.optimization_barrier(jnp.sum(d_norm * scaled, axis=0))
    stacked = jnp.concatenate([d_gate, d_up], axis=1)

    def token_step(index, total):
        first = (index * TOK_DEV).astype(jnp.int32)
        rows = lax.dynamic_slice_in_dim(normed, first, TOK_DEV, 0)
        grads = lax.dynamic_slice_in_dim(stacked, first, TOK_DEV, 0)
        term = lax.dot_general(rows, grads, (((0,), (0,)), ((), ())), preferred_element_type=jnp.float32)
        term = lax.optimization_barrier(term.astype(jnp.bfloat16)).astype(jnp.float32)
        return total + term
    both = lax.fori_loop(0, N_DP, token_step, jnp.zeros((D, 2 * FF), jnp.float32))
    return (d_gain, both[:, :FF], both[:, FF:])

def reference(tokens, norm_gain, w_gate, w_up, cotangent, decay_mask, radius):
    values = tokens.astype(jnp.float32)
    scaled = values * lax.rsqrt(lax.optimization_barrier(jnp.mean(values * values, axis=1, keepdims=True)) + 1e-06)
    asc_gain, asc_gate_f, asc_up_f = pass_grads(scaled, norm_gain, w_gate, w_up, cotangent)
    asc_gate = asc_gate_f.astype(jnp.bfloat16).astype(jnp.float32)
    asc_up = asc_up_f.astype(jnp.bfloat16).astype(jnp.float32)
    groups = decay_mask.astype(jnp.float32)
    gate_rows = groups[0][:, None]
    up_rows = groups[1][:, None]
    total = jnp.sum(gate_rows * asc_gate * asc_gate) + jnp.sum(up_rows * asc_up * asc_up)
    factor = radius[0] / (jnp.sqrt(total) + 1e-12)
    new_gate = (w_gate.astype(jnp.float32) + factor * gate_rows * asc_gate).astype(jnp.bfloat16)
    new_up = (w_up.astype(jnp.float32) + factor * up_rows * asc_up).astype(jnp.bfloat16)
    grad_gain, grad_gate, grad_up = pass_grads(scaled, norm_gain, new_gate, new_up, cotangent)
    return (grad_gain, grad_gate, grad_up)
```

```python
import functools

import jax
import jax.numpy as jnp
from jax import lax
from jax.experimental import pallas as pl
from jax.experimental.pallas import tpu as pltpu
from jax.sharding import PartitionSpec as P

MESH = pl.DeviceIdType.MESH


def remote(src, dst, send_sem, recv_sem, target):
    return pltpu.make_async_remote_copy(
        src_ref=src,
        dst_ref=dst,
        send_sem=send_sem,
        recv_sem=recv_sem,
        device_id=target,
        device_id_type=MESH,
    )


def greet(targets):
    barrier = pltpu.get_barrier_semaphore()
    for target in targets:
        pl.semaphore_signal(barrier, inc=1, device_id=target, device_id_type=MESH)
    pl.semaphore_wait(barrier, len(targets))


def dp_peers(n, d, q):
    return [(lax.rem(d + k, n), q) for k in range(1, n)]


def mp_peers(m, d, q):
    return [(d, lax.rem(q + k, m)) for k in range(1, m)]


def spread_kernel(
    n, x_ref, w_ref, k_ref, xs, ws, ks, x_send, x_recv, w_send, w_recv, k_send, k_recv, own_sem
):
    d, q = lax.axis_index("dp"), lax.axis_index("mp")
    rows, feats = x_ref.shape
    depth = w_ref.shape[1]
    zs = n // 2
    z, y = d // 2, lax.rem(d, 2)
    x, c = q // 2, lax.rem(q, 2)
    other_y, other_x, other_c = (2 * z + 1 - y, q), (d, 2 * (1 - x) + c), (d, 2 * x + 1 - c)
    greet(dp_peers(n, d, q) + [other_x, other_c])

    def block(dd, qq):
        return xs.at[
            pl.ds(pl.multiple_of(dd * rows, rows), rows), pl.ds(pl.multiple_of(qq * feats, feats), feats)
        ]

    def w_rows(dd):
        return ws.at[pl.ds(pl.multiple_of(dd * depth, depth), depth)]

    started = []

    def push(src, dd, qq, target):
        copy = remote(src, block(dd, qq), x_send.at[len(started)], x_recv.at[dd, qq], target)
        copy.start()
        started.append(copy)

    def arrive(dd, qq):
        remote(block(dd, qq), block(dd, qq), x_send.at[0], x_recv.at[dd, qq], other_c).wait_recv()

    own = [
        pltpu.make_async_copy(x_ref, block(d, q), own_sem.at[0]),
        pltpu.make_async_copy(w_ref.at[d], w_rows(d), own_sem.at[1]),
        pltpu.make_async_copy(k_ref.at[d], ks.at[d], own_sem.at[2]),
    ]
    for k in range(1, zs):
        push(x_ref, d, q, (2 * lax.rem(z + k, zs) + y, q))
    for target in (other_y, other_x, other_c):
        push(x_ref, d, q, target)
    for copy in own:
        copy.start()
    for k in range(1, zs):
        dd = 2 * lax.rem(z + zs - k, zs) + y
        arrive(dd, q)
        for target in (other_y, other_x, other_c):
            push(block(dd, q), dd, q, target)
    moves = []
    for k, (dd, qq) in enumerate(dp_peers(n, d, q)):
        moves.append(remote(w_ref.at[dd], w_rows(d), w_send.at[k], w_recv.at[d], (dd, qq)))
        moves.append(remote(k_ref.at[dd], ks.at[d], k_send.at[k], k_recv.at[d], (dd, qq)))
    for copy in moves:
        copy.start()
    for k in range(zs):
        dd = 2 * lax.rem(z + zs - k, zs) + 1 - y
        arrive(dd, q)
        for target in (other_x, other_c):
            push(block(dd, q), dd, q, target)
    y_order = [2 * lax.rem(z + zs - k, zs) + (y if side == 0 else 1 - y) for side in (0, 1) for k in range(zs)]
    for dd in y_order:
        arrive(dd, other_x[1])
        push(block(dd, other_x[1]), dd, other_x[1], other_c)
    for qq in (other_c[1], 2 * (1 - x) + 1 - c):
        for dd in y_order:
            arrive(dd, qq)
    for dd, _ in dp_peers(n, d, q):
        remote(w_rows(dd), w_rows(dd), w_send.at[0], w_recv.at[dd], other_c).wait_recv()
        remote(ks.at[dd], ks.at[dd], k_send.at[0], k_recv.at[dd], other_c).wait_recv()
    for copy in started + moves:
        copy.wait_send()
    for copy in own:
        copy.wait()


def spread(n, m, x, w, k):
    anywhere = pl.BlockSpec(memory_space=pl.ANY)
    return pl.pallas_call(
        functools.partial(spread_kernel, n),
        out_shape=(
            jax.ShapeDtypeStruct((n * x.shape[0], m * x.shape[1]), x.dtype),
            jax.ShapeDtypeStruct((n * w.shape[1], w.shape[2]), w.dtype),
            jax.ShapeDtypeStruct(k.shape, k.dtype),
        ),
        in_specs=[anywhere] * 3,
        out_specs=(anywhere,) * 3,
        scratch_shapes=[
            pltpu.SemaphoreType.DMA((n * m - 1,)),
            pltpu.SemaphoreType.DMA((n, m)),
            pltpu.SemaphoreType.DMA((n - 1,)),
            pltpu.SemaphoreType.DMA((n,)),
            pltpu.SemaphoreType.DMA((n - 1,)),
            pltpu.SemaphoreType.DMA((n,)),
            pltpu.SemaphoreType.DMA((3,)),
        ],
        compiler_params=pltpu.CompilerParams(collective_id=0, has_side_effects=True),
        name="spread",
    )(x, w, k)


def total_kernel(n, m, part_ref, sum_ref, dp_slots, mp_slots, dp_send, dp_recv, mp_send, mp_recv):
    d, q = lax.axis_index("dp"), lax.axis_index("mp")
    over_dp, over_mp = dp_peers(n, d, q), mp_peers(m, d, q)
    greet(over_dp + over_mp)
    sum_over(d, over_dp, part_ref, part_ref, dp_slots, dp_send, dp_recv)
    column = functools.reduce(lambda a, b: a + b, [dp_slots[i] for i in range(n)])
    mp_slots[q] = column
    sends = [remote(mp_slots.at[q], mp_slots.at[q], mp_send.at[k], mp_recv.at[q], t) for k, t in enumerate(over_mp)]
    for copy in sends:
        copy.start()
    for _, qq in over_mp:
        remote(mp_slots.at[qq], mp_slots.at[qq], mp_send.at[0], mp_recv.at[qq], over_mp[0]).wait_recv()
    for copy in sends:
        copy.wait_send()
    sum_ref[...] = functools.reduce(lambda a, b: a + b, [mp_slots[i] for i in range(m)])


def sum_over(d, peers, part_ref, own_ref, slots, send, recv):
    slots[d] = own_ref[...]
    sends = [remote(part_ref, slots.at[d], send.at[k], recv.at[d], t) for k, t in enumerate(peers)]
    for copy in sends:
        copy.start()
    for dd, _ in peers:
        remote(slots.at[dd], slots.at[dd], send.at[0], recv.at[dd], peers[0]).wait_recv()
    for copy in sends:
        copy.wait_send()


def total_sum(n, m, part):
    return pl.pallas_call(
        functools.partial(total_kernel, n, m),
        out_shape=jax.ShapeDtypeStruct(part.shape, part.dtype),
        in_specs=[pl.BlockSpec(memory_space=pltpu.VMEM)],
        out_specs=pl.BlockSpec(memory_space=pltpu.VMEM),
        scratch_shapes=[
            pltpu.VMEM((n,) + part.shape, part.dtype),
            pltpu.VMEM((m,) + part.shape, part.dtype),
            pltpu.SemaphoreType.DMA((n - 1,)),
            pltpu.SemaphoreType.DMA((n,)),
            pltpu.SemaphoreType.DMA((m - 1,)),
            pltpu.SemaphoreType.DMA((m,)),
        ],
        compiler_params=pltpu.CompilerParams(collective_id=1, has_side_effects=True),
        name="total_sum",
    )(part)


def collect_kernel(
    n, m, g_ref, part_ref, gs, gain_ref, dp_slots, sums, mp_slots,
    g_send, g_recv, dp_send, dp_recv, mp_send, mp_recv, own_sem,
):
    d, q = lax.axis_index("dp"), lax.axis_index("mp")
    over_dp, over_mp = dp_peers(n, d, q), mp_peers(m, d, q)
    greet(over_dp + over_mp)
    moves = [remote(g_ref.at[t[0]], gs.at[d], g_send.at[k], g_recv.at[d], t) for k, t in enumerate(over_dp)]
    own = pltpu.make_async_copy(g_ref.at[d], gs.at[d], own_sem)
    for copy in moves:
        copy.start()
    own.start()
    sum_over(d, over_dp, part_ref, part_ref, dp_slots, dp_send, dp_recv)
    sums[...] = functools.reduce(lambda a, b: a + b, [dp_slots[i] for i in range(n)])
    mp_slots[q] = sums[q]
    sends = [remote(sums.at[t[1]], mp_slots.at[q], mp_send.at[k], mp_recv.at[q], t) for k, t in enumerate(over_mp)]
    for copy in sends:
        copy.start()
    for _, qq in over_mp:
        remote(mp_slots.at[qq], mp_slots.at[qq], mp_send.at[0], mp_recv.at[qq], over_mp[0]).wait_recv()
    for copy in sends:
        copy.wait_send()
    gain_ref[...] = functools.reduce(lambda a, b: a + b, [mp_slots[i] for i in range(m)])
    for dd, _ in over_dp:
        remote(gs.at[dd], gs.at[dd], g_send.at[0], g_recv.at[dd], over_dp[0]).wait_recv()
    for copy in moves:
        copy.wait_send()
    own.wait()


def collect(n, m, g, part):
    anywhere = pl.BlockSpec(memory_space=pl.ANY)
    inside = pl.BlockSpec(memory_space=pltpu.VMEM)
    return pl.pallas_call(
        functools.partial(collect_kernel, n, m),
        out_shape=(
            jax.ShapeDtypeStruct(g.shape, g.dtype),
            jax.ShapeDtypeStruct(part.shape[1:], part.dtype),
        ),
        in_specs=[anywhere, inside],
        out_specs=(anywhere, inside),
        scratch_shapes=[
            pltpu.VMEM((n,) + part.shape, part.dtype),
            pltpu.VMEM(part.shape, part.dtype),
            pltpu.VMEM(part.shape, part.dtype),
            pltpu.SemaphoreType.DMA((n - 1,)),
            pltpu.SemaphoreType.DMA((n,)),
            pltpu.SemaphoreType.DMA((n - 1,)),
            pltpu.SemaphoreType.DMA((n,)),
            pltpu.SemaphoreType.DMA((m - 1,)),
            pltpu.SemaphoreType.DMA((m,)),
            pltpu.SemaphoreType.DMA,
        ],
        compiler_params=pltpu.CompilerParams(collective_id=2, has_side_effects=True),
        name="collect",
    )(g, part)


def column_pass(normed, both, upstream):
    cols = both.shape[1] // 2
    pre = jnp.dot(normed, both, preferred_element_type=jnp.float32)
    activated, back_fn = jax.vjp(activation, pre[:, :cols])
    d_up = (upstream * activated).astype(jnp.bfloat16)
    d_gate = back_fn(upstream * pre[:, cols:])[0].astype(jnp.bfloat16)
    stacked = jnp.concatenate([d_gate, d_up], axis=1)
    return lax.dot_general(normed, stacked, (((0,), (0,)), ((), ())), preferred_element_type=jnp.float32)


def column_body(tokens, norm_gain, w_gate, w_up, cotangent, decay_mask, radius):
    n, m = lax.axis_size("dp"), lax.axis_size("mp")
    rows, feats = tokens.shape
    depth, width = w_gate.shape
    cols = width // n
    values = tokens.astype(jnp.float32)
    row_total = lax.psum(jnp.sum(values * values, axis=1), "mp")
    scaled = values * lax.rsqrt(row_total / (feats * m) + 1e-06)[:, None]
    normed_part = (scaled * norm_gain[None, :]).astype(jnp.bfloat16)

    def by_owner(part):
        return part.reshape(part.shape[0], n, cols).transpose(1, 0, 2)

    w_blocks = jnp.concatenate([by_owner(w_gate), by_owner(w_up)], axis=2)
    cot_blocks = by_owner(cotangent)
    cot_blocks = jnp.concatenate([cot_blocks[:, : rows // 2], cot_blocks[:, rows // 2 :]], axis=2)
    normed, both, cot = spread(n, m, normed_part, w_blocks, cot_blocks)
    upstream = jnp.concatenate([cot[:, :, :cols], cot[:, :, cols:]], axis=1)
    upstream = upstream.reshape(n * rows, cols).astype(jnp.float32)

    groups = decay_mask.astype(jnp.float32)
    is_gate = lax.broadcasted_iota(jnp.int32, (1, 2 * cols), 1) < cols
    mask = jnp.where(is_gate, groups[0][:, None], groups[1][:, None])
    asc = column_pass(normed, both, upstream).astype(jnp.bfloat16).astype(jnp.float32)
    part = jnp.sum(mask * asc * asc)
    total = total_sum(n, m, jnp.full((8, 128), part, jnp.float32))[0, 0]
    factor = radius[0] / (jnp.sqrt(total) + 1e-12)
    moved = (both.astype(jnp.float32) + factor * mask * asc).astype(jnp.bfloat16)

    grads = column_pass(normed, moved, upstream)
    gain_part = jnp.sum(moved.astype(jnp.float32) * grads, axis=1)
    grads = grads.astype(jnp.bfloat16).reshape(n, depth, 2 * cols)
    grads, gain_sum = collect(n, m, grads, gain_part.reshape(m, 8, feats // 8))
    grads = grads.transpose(1, 0, 2).astype(jnp.float32)
    d_gain = gain_sum.reshape(feats) / norm_gain
    return (
        d_gain,
        grads[:, :, :cols].reshape(depth, width),
        grads[:, :, cols:].reshape(depth, width),
    )


def activation(value):
    return jax.nn.gelu(value, approximate=True)


def fetch_weights(part_gate, part_up):
    return (
        lax.all_gather(part_gate, "dp", axis=0, tiled=True),
        lax.all_gather(part_up, "dp", axis=0, tiled=True),
    )


def one_pass(scaled_rows, gain_part, full_gate, full_up, cotangent):
    hidden_width = full_gate.shape[1]
    normed_part = (scaled_rows * gain_part[None, :]).astype(jnp.bfloat16)
    normed = lax.all_gather(normed_part, "mp", axis=1, tiled=True)
    pre_gate = jnp.dot(normed, full_gate, preferred_element_type=jnp.float32)
    pre_up = jnp.dot(normed, full_up, preferred_element_type=jnp.float32)
    activated, back_fn = jax.vjp(activation, pre_gate)
    upstream = cotangent.astype(jnp.float32)
    d_up = (upstream * activated).astype(jnp.bfloat16)
    d_gate = back_fn(upstream * pre_up)[0].astype(jnp.bfloat16)
    feature_term = lax.dot_general(
        d_gate, full_gate, (((1,), (1,)), ((), ())), preferred_element_type=jnp.float32
    )
    feature_term = feature_term + lax.dot_general(
        d_up, full_up, (((1,), (1,)), ((), ())), preferred_element_type=jnp.float32
    )
    d_norm = lax.psum_scatter(
        feature_term.astype(jnp.bfloat16), "mp", scatter_dimension=1, tiled=True
    ).astype(jnp.float32)
    d_gain = lax.psum(jnp.sum(d_norm * scaled_rows, axis=0), "dp")
    stacked = jnp.concatenate([d_gate, d_up], axis=1)
    both = lax.psum_scatter(
        lax.dot_general(
            normed, stacked, (((0,), (0,)), ((), ())), preferred_element_type=jnp.float32
        ).astype(jnp.bfloat16),
        "dp",
        scatter_dimension=0,
        tiled=True,
    ).astype(jnp.float32)
    return (d_gain, both[:, :hidden_width], both[:, hidden_width:])


def body(tokens, norm_gain, w_gate, w_up, cotangent, decay_mask, radius):
    values = tokens.astype(jnp.float32)
    width = values.shape[1] * lax.axis_size("mp")
    row_total = lax.psum(jnp.sum(values * values, axis=1), "mp")
    scaled_rows = values * lax.rsqrt(row_total / width + 1e-06)[:, None]
    groups = decay_mask.astype(jnp.float32)
    local_rows = w_gate.shape[0]
    first_row = lax.axis_index("dp") * local_rows
    local_groups = lax.dynamic_slice_in_dim(groups, first_row, local_rows, 1)
    gate_mask = local_groups[0][:, None]
    up_mask = local_groups[1][:, None]
    full_gate, full_up = fetch_weights(w_gate, w_up)
    asc_gain, asc_gate_f, asc_up_f = one_pass(scaled_rows, norm_gain, full_gate, full_up, cotangent)
    gate_low = asc_gate_f.astype(jnp.bfloat16)
    up_low = asc_up_f.astype(jnp.bfloat16)
    gate_wide = gate_low.astype(jnp.float32)
    up_wide = up_low.astype(jnp.float32)
    matrix_part = jnp.sum(gate_mask * gate_wide * gate_wide) + jnp.sum(up_mask * up_wide * up_wide)
    total = lax.psum(matrix_part, ("dp", "mp"))
    factor = radius[0] / (jnp.sqrt(total) + 1e-12)
    new_gate = (w_gate.astype(jnp.float32) + factor * gate_mask * gate_wide).astype(jnp.bfloat16)
    new_up = (w_up.astype(jnp.float32) + factor * up_mask * up_wide).astype(jnp.bfloat16)
    next_gate, next_up = fetch_weights(new_gate, new_up)
    return one_pass(scaled_rows, norm_gain, next_gate, next_up, cotangent)


def either_body(tokens, norm_gain, w_gate, *rest):
    n, m = lax.axis_size("dp"), lax.axis_size("mp")
    by_columns = m == 4 and n % 2 == 0 and (2 * w_gate.shape[1]) % (128 * n) == 0
    return (column_body if by_columns else body)(tokens, norm_gain, w_gate, *rest)


def solution(mesh):
    placed = (P("dp", "mp"), P("mp"), P("dp", "mp"), P("dp", "mp"), P("dp", "mp"), P(), P())
    return jax.shard_map(
        either_body,
        mesh=mesh,
        in_specs=placed,
        out_specs=(P("mp"), P("dp", "mp"), P("dp", "mp")),
        check_vma=False,
    )
```

```python
import functools

import jax
import jax.numpy as jnp
from jax import lax
from jax.experimental import pallas as pl
from jax.experimental.pallas import tpu as pltpu
from jax.sharding import PartitionSpec as P

MESH = pl.DeviceIdType.MESH
LANES = 128


def remote(src, dst, send_sem, recv_sem, target):
    return pltpu.make_async_remote_copy(
        src_ref=src,
        dst_ref=dst,
        send_sem=send_sem,
        recv_sem=recv_sem,
        device_id=target,
        device_id_type=MESH,
    )


def greet(targets):
    barrier = pltpu.get_barrier_semaphore()
    for target in targets:
        pl.semaphore_signal(barrier, inc=1, device_id=target, device_id_type=MESH)
    pl.semaphore_wait(barrier, len(targets))


def dp_peers(n, d, q):
    return [(lax.rem(d + k, n), q) for k in range(1, n)]


def mp_peers(m, d, q):
    return [(d, lax.rem(q + k, m)) for k in range(1, m)]


def spread_kernel(
    n, x_ref, w_ref, k_ref, xs, ws, ks, z_send, x_send, x_recv, w_send, w_recv, k_send, k_recv, own_sem
):
    d, q = lax.axis_index("dp"), lax.axis_index("mp")
    rows, feats = x_ref.shape
    depth = w_ref.shape[1]
    zs = n // 2
    z, y = d // 2, lax.rem(d, 2)
    x, c = q // 2, lax.rem(q, 2)
    other_y, other_x, other_c = (2 * z + 1 - y, q), (d, 2 * (1 - x) + c), (d, 2 * x + 1 - c)
    greet(dp_peers(n, d, q) + [other_x, other_c])

    def block(dd, qq):
        return xs.at[
            pl.ds(pl.multiple_of(dd * rows, rows), rows), pl.ds(pl.multiple_of(qq * feats, feats), feats)
        ]

    def w_rows(dd):
        return ws.at[pl.ds(pl.multiple_of(dd * depth, depth), depth)]

    targets = (other_y, other_x, other_c)

    def hop(src, kind, dd, qq):
        return remote(src, block(dd, qq), x_send.at[kind, dd, qq], x_recv.at[dd, qq], targets[kind])

    def push(src, kinds, dd, qq):
        for kind in kinds:
            hop(src, kind, dd, qq).start()

    def arrive(dd, qq):
        remote(block(dd, qq), block(dd, qq), x_send.at[2, dd, qq], x_recv.at[dd, qq], other_c).wait_recv()

    own = [
        pltpu.make_async_copy(x_ref, block(d, q), own_sem.at[0]),
        pltpu.make_async_copy(w_ref.at[d], w_rows(d), own_sem.at[1]),
        pltpu.make_async_copy(k_ref.at[d], ks.at[d], own_sem.at[2]),
    ]

    def along_z(step, k):
        origin, target = z - step * k, z + step
        here = jnp.logical_and(origin >= 0, origin < zs)
        onward = jnp.logical_and(here, jnp.logical_and(target >= 0, target < zs))
        dd = 2 * lax.rem(origin + zs, zs) + y
        target = (2 * lax.rem(target + zs, zs) + y, q)
        src = x_ref if k == 0 else block(dd, q)
        copy = remote(src, block(dd, q), z_send.at[(step + 1) // 2, k], x_recv.at[dd, q], target)
        return here, onward, dd, copy

    def forward(step, k):
        here, onward, dd, copy = along_z(step, k)
        if k > 0:
            pl.when(here)(lambda: arrive(dd, q))
        pl.when(onward)(lambda: copy.start())
        if k > 0:
            pl.when(here)(lambda: push(block(dd, q), (0, 1, 2), dd, q))

    for step in (1, -1):
        forward(step, 0)
    push(x_ref, (0, 1, 2), d, q)
    for copy in own:
        copy.start()
    for k in range(1, zs):
        for step in (1, -1):
            forward(step, k)
    moves = []
    for k, (dd, qq) in enumerate(dp_peers(n, d, q)):
        moves.append(remote(w_ref.at[dd], w_rows(d), w_send.at[k], w_recv.at[d], (dd, qq)))
        moves.append(remote(k_ref.at[dd], ks.at[d], k_send.at[k], k_recv.at[d], (dd, qq)))
    for copy in moves:
        copy.start()
    for k in range(zs):
        dd = 2 * lax.rem(z + zs - k, zs) + 1 - y
        arrive(dd, q)
        push(block(dd, q), (1, 2), dd, q)
    y_order = [2 * lax.rem(z + zs - k, zs) + (y if side == 0 else 1 - y) for side in (0, 1) for k in range(zs)]
    for dd in y_order:
        arrive(dd, other_x[1])
        push(block(dd, other_x[1]), (2,), dd, other_x[1])
    for qq in (other_c[1], 2 * (1 - x) + 1 - c):
        for dd in y_order:
            arrive(dd, qq)
    for dd, _ in dp_peers(n, d, q):
        remote(w_rows(dd), w_rows(dd), w_send.at[0], w_recv.at[dd], other_c).wait_recv()
        remote(ks.at[dd], ks.at[dd], k_send.at[0], k_recv.at[dd], other_c).wait_recv()
    for copy in moves:
        copy.wait_send()
    for dd in y_order:
        hop(block(dd, q), 1, dd, q).wait_send()
        for qq in (q, other_x[1]):
            hop(block(dd, qq), 2, dd, qq).wait_send()
    for dd in y_order[:zs]:
        hop(block(dd, q), 0, dd, q).wait_send()
    for k in range(zs):
        for step in (1, -1):
            _, onward, _, copy = along_z(step, k)
            pl.when(onward)(lambda copy=copy: copy.wait_send())
    for copy in own:
        copy.wait()


def spread(n, m, x, w, k):
    anywhere = pl.BlockSpec(memory_space=pl.ANY)
    return pl.pallas_call(
        functools.partial(spread_kernel, n),
        out_shape=(
            jax.ShapeDtypeStruct((n * x.shape[0], m * x.shape[1]), x.dtype),
            jax.ShapeDtypeStruct((n * w.shape[1], w.shape[2]), w.dtype),
            jax.ShapeDtypeStruct(k.shape, k.dtype),
        ),
        in_specs=[anywhere] * 3,
        out_specs=(anywhere,) * 3,
        scratch_shapes=[
            pltpu.SemaphoreType.DMA((2, n // 2)),
            pltpu.SemaphoreType.DMA((3, n, m)),
            pltpu.SemaphoreType.DMA((n, m)),
            pltpu.SemaphoreType.DMA((n - 1,)),
            pltpu.SemaphoreType.DMA((n,)),
            pltpu.SemaphoreType.DMA((n - 1,)),
            pltpu.SemaphoreType.DMA((n,)),
            pltpu.SemaphoreType.DMA((3,)),
        ],
        compiler_params=pltpu.CompilerParams(collective_id=0, has_side_effects=True),
        name="spread",
    )(x, w, k)


def total_kernel(n, m, part_ref, sum_ref, dp_slots, mp_slots, dp_send, dp_recv, mp_send, mp_recv):
    d, q = lax.axis_index("dp"), lax.axis_index("mp")
    over_dp, over_mp = dp_peers(n, d, q), mp_peers(m, d, q)
    greet(over_dp + over_mp)
    sum_over(d, over_dp, part_ref, part_ref, dp_slots, dp_send, dp_recv)
    column = functools.reduce(lambda a, b: a + b, [dp_slots[i] for i in range(n)])
    mp_slots[q] = column
    sends = [remote(mp_slots.at[q], mp_slots.at[q], mp_send.at[k], mp_recv.at[q], t) for k, t in enumerate(over_mp)]
    for copy in sends:
        copy.start()
    for _, qq in over_mp:
        remote(mp_slots.at[qq], mp_slots.at[qq], mp_send.at[0], mp_recv.at[qq], over_mp[0]).wait_recv()
    for copy in sends:
        copy.wait_send()
    sum_ref[...] = functools.reduce(lambda a, b: a + b, [mp_slots[i] for i in range(m)])


def sum_over(d, peers, part_ref, own_ref, slots, send, recv):
    slots[d] = own_ref[...]
    sends = [remote(part_ref, slots.at[d], send.at[k], recv.at[d], t) for k, t in enumerate(peers)]
    for copy in sends:
        copy.start()
    for dd, _ in peers:
        remote(slots.at[dd], slots.at[dd], send.at[0], recv.at[dd], peers[0]).wait_recv()
    for copy in sends:
        copy.wait_send()


def total_sum(n, m, part):
    return pl.pallas_call(
        functools.partial(total_kernel, n, m),
        out_shape=jax.ShapeDtypeStruct(part.shape, part.dtype),
        in_specs=[pl.BlockSpec(memory_space=pltpu.VMEM)],
        out_specs=pl.BlockSpec(memory_space=pltpu.VMEM),
        scratch_shapes=[
            pltpu.VMEM((n,) + part.shape, part.dtype),
            pltpu.VMEM((m,) + part.shape, part.dtype),
            pltpu.SemaphoreType.DMA((n - 1,)),
            pltpu.SemaphoreType.DMA((n,)),
            pltpu.SemaphoreType.DMA((m - 1,)),
            pltpu.SemaphoreType.DMA((m,)),
        ],
        compiler_params=pltpu.CompilerParams(collective_id=1, has_side_effects=True),
        name="total_sum",
    )(part)


def collect_kernel(
    n, m, g_ref, part_ref, gs, gain_ref, dp_slots, sums, mp_slots,
    g_send, g_recv, dp_send, dp_recv, mp_send, mp_recv, own_sem,
):
    d, q = lax.axis_index("dp"), lax.axis_index("mp")
    over_dp, over_mp = dp_peers(n, d, q), mp_peers(m, d, q)
    greet(over_dp + over_mp)
    moves = [remote(g_ref.at[t[0]], gs.at[d], g_send.at[k], g_recv.at[d], t) for k, t in enumerate(over_dp)]
    own = pltpu.make_async_copy(g_ref.at[d], gs.at[d], own_sem)
    for copy in moves:
        copy.start()
    own.start()
    sum_over(d, over_dp, part_ref, part_ref, dp_slots, dp_send, dp_recv)
    sums[...] = functools.reduce(lambda a, b: a + b, [dp_slots[i] for i in range(n)])
    mp_slots[q] = sums[q]
    sends = [remote(sums.at[t[1]], mp_slots.at[q], mp_send.at[k], mp_recv.at[q], t) for k, t in enumerate(over_mp)]
    for copy in sends:
        copy.start()
    for _, qq in over_mp:
        remote(mp_slots.at[qq], mp_slots.at[qq], mp_send.at[0], mp_recv.at[qq], over_mp[0]).wait_recv()
    for copy in sends:
        copy.wait_send()
    gain_ref[...] = functools.reduce(lambda a, b: a + b, [mp_slots[i] for i in range(m)])
    for dd, _ in over_dp:
        remote(gs.at[dd], gs.at[dd], g_send.at[0], g_recv.at[dd], over_dp[0]).wait_recv()
    for copy in moves:
        copy.wait_send()
    own.wait()


def collect(n, m, g, part):
    anywhere = pl.BlockSpec(memory_space=pl.ANY)
    inside = pl.BlockSpec(memory_space=pltpu.VMEM)
    return pl.pallas_call(
        functools.partial(collect_kernel, n, m),
        out_shape=(
            jax.ShapeDtypeStruct(g.shape, g.dtype),
            jax.ShapeDtypeStruct(part.shape[1:], part.dtype),
        ),
        in_specs=[anywhere, inside],
        out_specs=(anywhere, inside),
        scratch_shapes=[
            pltpu.VMEM((n,) + part.shape, part.dtype),
            pltpu.VMEM(part.shape, part.dtype),
            pltpu.VMEM(part.shape, part.dtype),
            pltpu.SemaphoreType.DMA((n - 1,)),
            pltpu.SemaphoreType.DMA((n,)),
            pltpu.SemaphoreType.DMA((n - 1,)),
            pltpu.SemaphoreType.DMA((n,)),
            pltpu.SemaphoreType.DMA((m - 1,)),
            pltpu.SemaphoreType.DMA((m,)),
            pltpu.SemaphoreType.DMA,
        ],
        compiler_params=pltpu.CompilerParams(collective_id=2, has_side_effects=True),
        name="collect",
    )(g, part)


def swap_halves(tile):
    return pltpu.roll(tile, LANES // 2, 1)


def by_owner_kernel(a_ref, b_ref, out_ref):
    left = lax.broadcasted_iota(jnp.int32, (a_ref.shape[0], LANES), 1) < LANES // 2
    for p in range(out_ref.shape[0] // 2):
        first, middle, last = (pl.ds((3 * p + i) * LANES, LANES) for i in range(3))
        a_mid = a_ref[:, middle].astype(jnp.float32)
        b_mid = b_ref[:, middle].astype(jnp.float32)
        out_ref[2 * p, :, :LANES] = a_ref[:, first]
        out_ref[2 * p, :, LANES : 2 * LANES] = jnp.where(left, a_mid, swap_halves(b_mid)).astype(out_ref.dtype)
        out_ref[2 * p, :, 2 * LANES :] = b_ref[:, first]
        out_ref[2 * p + 1, :, :LANES] = a_ref[:, last]
        out_ref[2 * p + 1, :, LANES : 2 * LANES] = jnp.where(left, swap_halves(a_mid), b_mid).astype(out_ref.dtype)
        out_ref[2 * p + 1, :, 2 * LANES :] = b_ref[:, last]


def by_owner(n, a, b, rows, b_from=0):
    step = min(rows, 128)
    width = a.shape[1]
    return pl.pallas_call(
        by_owner_kernel,
        grid=(rows // step,),
        out_shape=jax.ShapeDtypeStruct((n, rows, 3 * LANES), a.dtype),
        in_specs=[
            pl.BlockSpec((step, width), lambda i: (i, 0)),
            pl.BlockSpec((step, width), lambda i: (i + b_from // step, 0)),
        ],
        out_specs=pl.BlockSpec((n, step, 3 * LANES), lambda i: (0, i, 0)),
        compiler_params=pltpu.CompilerParams(vmem_limit_bytes=24 * 2**20),
        name="by_owner",
    )(a, b)


def in_place_kernel(g_ref, gate_ref, up_ref):
    left = lax.broadcasted_iota(jnp.int32, (g_ref.shape[1], LANES), 1) < LANES // 2
    for p in range(g_ref.shape[0] // 2):
        first, middle, last = (pl.ds((3 * p + i) * LANES, LANES) for i in range(3))
        one = g_ref[2 * p].astype(jnp.float32)
        two = g_ref[2 * p + 1].astype(jnp.float32)
        one_mid, two_mid = one[:, LANES : 2 * LANES], two[:, LANES : 2 * LANES]
        gate_ref[:, first] = one[:, :LANES]
        gate_ref[:, middle] = jnp.where(left, one_mid, swap_halves(two_mid))
        gate_ref[:, last] = two[:, :LANES]
        up_ref[:, first] = one[:, 2 * LANES :]
        up_ref[:, middle] = jnp.where(left, swap_halves(one_mid), two_mid)
        up_ref[:, last] = two[:, 2 * LANES :]


def in_place(g, width):
    n, rows, share = g.shape
    step = 64
    whole = pl.BlockSpec((step, width), lambda i: (i, 0))
    return pl.pallas_call(
        in_place_kernel,
        grid=(rows // step,),
        out_shape=(jax.ShapeDtypeStruct((rows, width), jnp.float32),) * 2,
        in_specs=[pl.BlockSpec((n, step, share), lambda i: (0, i, 0))],
        out_specs=(whole, whole),
        compiler_params=pltpu.CompilerParams(vmem_limit_bytes=24 * 2**20),
        name="in_place",
    )(g)


def column_pass(normed, both, upstream):
    cols = both.shape[1] // 2
    pre = jnp.dot(normed, both, preferred_element_type=jnp.float32)
    pre_up = jnp.concatenate([pre[:, 2 * LANES :], pre[:, cols : 2 * LANES]], axis=1)
    activated, back_fn = jax.vjp(activation, pre[:, :cols])
    d_up = (upstream * activated).astype(jnp.bfloat16)
    d_gate = back_fn(upstream * pre_up)[0].astype(jnp.bfloat16)
    stacked = jnp.concatenate([d_gate, d_up[:, LANES:], d_up[:, :LANES]], axis=1)
    return lax.dot_general(normed, stacked, (((0,), (0,)), ((), ())), preferred_element_type=jnp.float32)


def column_body(tokens, norm_gain, w_gate, w_up, cotangent, decay_mask, radius):
    n, m = lax.axis_size("dp"), lax.axis_size("mp")
    rows, feats = tokens.shape
    depth, width = w_gate.shape
    cols = width // n
    values = tokens.astype(jnp.float32)
    row_total = lax.psum(jnp.sum(values * values, axis=1), "mp")
    scaled = values * lax.rsqrt(row_total / (feats * m) + 1e-06)[:, None]
    normed_part = (scaled * norm_gain[None, :]).astype(jnp.bfloat16)

    w_blocks = by_owner(n, w_gate, w_up, depth)
    cot_blocks = by_owner(n, cotangent, cotangent, rows // 2, rows // 2)
    normed, both, cot = spread(n, m, normed_part, w_blocks, cot_blocks)
    whole_tile = jnp.concatenate([cot[:, :, :LANES], cot[:, :, 2 * LANES :]], axis=1)
    half_tile = jnp.concatenate([cot[:, :, LANES:cols], cot[:, :, cols : 2 * LANES]], axis=1)
    upstream = jnp.concatenate([whole_tile, half_tile], axis=2)
    upstream = upstream.reshape(n * rows, cols).astype(jnp.float32)

    groups = decay_mask.astype(jnp.float32)
    is_gate = lax.broadcasted_iota(jnp.int32, (1, 2 * cols), 1) < cols
    mask = jnp.where(is_gate, groups[0][:, None], groups[1][:, None])
    asc = column_pass(normed, both, upstream).astype(jnp.bfloat16).astype(jnp.float32)
    part = jnp.sum(mask * asc * asc)
    total = total_sum(n, m, jnp.full((8, 128), part, jnp.float32))[0, 0]
    factor = radius[0] / (jnp.sqrt(total) + 1e-12)
    moved = (both.astype(jnp.float32) + factor * mask * asc).astype(jnp.bfloat16)

    grads = column_pass(normed, moved, upstream)
    gain_part = jnp.sum(moved.astype(jnp.float32) * grads, axis=1)
    grads = grads.astype(jnp.bfloat16).reshape(n, depth, 2 * cols)
    grads, gain_sum = collect(n, m, grads, gain_part.reshape(m, 8, feats // 8))
    d_gain = gain_sum.reshape(feats) / norm_gain
    return (d_gain,) + tuple(in_place(grads, width))


def activation(value):
    return jax.nn.gelu(value, approximate=True)


def fetch_weights(part_gate, part_up):
    return (
        lax.all_gather(part_gate, "dp", axis=0, tiled=True),
        lax.all_gather(part_up, "dp", axis=0, tiled=True),
    )


def one_pass(scaled_rows, gain_part, full_gate, full_up, cotangent):
    hidden_width = full_gate.shape[1]
    normed_part = (scaled_rows * gain_part[None, :]).astype(jnp.bfloat16)
    normed = lax.all_gather(normed_part, "mp", axis=1, tiled=True)
    pre_gate = jnp.dot(normed, full_gate, preferred_element_type=jnp.float32)
    pre_up = jnp.dot(normed, full_up, preferred_element_type=jnp.float32)
    activated, back_fn = jax.vjp(activation, pre_gate)
    upstream = cotangent.astype(jnp.float32)
    d_up = (upstream * activated).astype(jnp.bfloat16)
    d_gate = back_fn(upstream * pre_up)[0].astype(jnp.bfloat16)
    feature_term = lax.dot_general(
        d_gate, full_gate, (((1,), (1,)), ((), ())), preferred_element_type=jnp.float32
    )
    feature_term = feature_term + lax.dot_general(
        d_up, full_up, (((1,), (1,)), ((), ())), preferred_element_type=jnp.float32
    )
    d_norm = lax.psum_scatter(
        feature_term.astype(jnp.bfloat16), "mp", scatter_dimension=1, tiled=True
    ).astype(jnp.float32)
    d_gain = lax.psum(jnp.sum(d_norm * scaled_rows, axis=0), "dp")
    stacked = jnp.concatenate([d_gate, d_up], axis=1)
    both = lax.psum_scatter(
        lax.dot_general(
            normed, stacked, (((0,), (0,)), ((), ())), preferred_element_type=jnp.float32
        ).astype(jnp.bfloat16),
        "dp",
        scatter_dimension=0,
        tiled=True,
    ).astype(jnp.float32)
    return (d_gain, both[:, :hidden_width], both[:, hidden_width:])


def body(tokens, norm_gain, w_gate, w_up, cotangent, decay_mask, radius):
    values = tokens.astype(jnp.float32)
    width = values.shape[1] * lax.axis_size("mp")
    row_total = lax.psum(jnp.sum(values * values, axis=1), "mp")
    scaled_rows = values * lax.rsqrt(row_total / width + 1e-06)[:, None]
    groups = decay_mask.astype(jnp.float32)
    local_rows = w_gate.shape[0]
    first_row = lax.axis_index("dp") * local_rows
    local_groups = lax.dynamic_slice_in_dim(groups, first_row, local_rows, 1)
    gate_mask = local_groups[0][:, None]
    up_mask = local_groups[1][:, None]
    full_gate, full_up = fetch_weights(w_gate, w_up)
    asc_gain, asc_gate_f, asc_up_f = one_pass(scaled_rows, norm_gain, full_gate, full_up, cotangent)
    gate_low = asc_gate_f.astype(jnp.bfloat16)
    up_low = asc_up_f.astype(jnp.bfloat16)
    gate_wide = gate_low.astype(jnp.float32)
    up_wide = up_low.astype(jnp.float32)
    matrix_part = jnp.sum(gate_mask * gate_wide * gate_wide) + jnp.sum(up_mask * up_wide * up_wide)
    total = lax.psum(matrix_part, ("dp", "mp"))
    factor = radius[0] / (jnp.sqrt(total) + 1e-12)
    new_gate = (w_gate.astype(jnp.float32) + factor * gate_mask * gate_wide).astype(jnp.bfloat16)
    new_up = (w_up.astype(jnp.float32) + factor * up_mask * up_wide).astype(jnp.bfloat16)
    next_gate, next_up = fetch_weights(new_gate, new_up)
    return one_pass(scaled_rows, norm_gain, next_gate, next_up, cotangent)


def either_body(tokens, norm_gain, w_gate, *rest):
    n, m = lax.axis_size("dp"), lax.axis_size("mp")
    by_columns = m == 4 and n % 2 == 0 and 2 * w_gate.shape[1] == 3 * LANES * n
    return (column_body if by_columns else body)(tokens, norm_gain, w_gate, *rest)


def solution(mesh):
    placed = (P("dp", "mp"), P("mp"), P("dp", "mp"), P("dp", "mp"), P("dp", "mp"), P(), P())
    return jax.shard_map(
        either_body,
        mesh=mesh,
        in_specs=placed,
        out_specs=(P("mp"), P("dp", "mp"), P("dp", "mp")),
        check_vma=False,
    )
```

```python
import functools

import jax
import jax.numpy as jnp
from jax import lax
from jax.experimental import pallas as pl
from jax.experimental.pallas import tpu as pltpu
from jax.sharding import PartitionSpec as P

MESH = pl.DeviceIdType.MESH
LANES = 128


def remote(src, dst, send_sem, recv_sem, target):
    return pltpu.make_async_remote_copy(
        src_ref=src,
        dst_ref=dst,
        send_sem=send_sem,
        recv_sem=recv_sem,
        device_id=target,
        device_id_type=MESH,
    )


def greet(targets):
    barrier = pltpu.get_barrier_semaphore()
    for target in targets:
        pl.semaphore_signal(barrier, inc=1, device_id=target, device_id_type=MESH)
    pl.semaphore_wait(barrier, len(targets))


def dp_peers(n, d, q):
    return [(lax.rem(d + k, n), q) for k in range(1, n)]


def mp_peers(m, d, q):
    return [(d, lax.rem(q + k, m)) for k in range(1, m)]


def spread_kernel(
    n, x_ref, w_ref, k_ref, xs, ws, ks, z_send, x_send, x_recv, w_send, w_recv, k_send, k_recv, own_sem
):
    d, q = lax.axis_index("dp"), lax.axis_index("mp")
    rows, feats = x_ref.shape
    depth = w_ref.shape[1]
    zs = n // 2
    z, y = d // 2, lax.rem(d, 2)
    x, c = q // 2, lax.rem(q, 2)
    other_y, other_x, other_c = (2 * z + 1 - y, q), (d, 2 * (1 - x) + c), (d, 2 * x + 1 - c)
    greet(dp_peers(n, d, q) + [other_x, other_c])

    def block(dd, qq):
        return xs.at[
            pl.ds(pl.multiple_of(dd * rows, rows), rows), pl.ds(pl.multiple_of(qq * feats, feats), feats)
        ]

    def w_rows(dd):
        return ws.at[pl.ds(pl.multiple_of(dd * depth, depth), depth)]

    targets = (other_y, other_x, other_c)

    def hop(src, kind, dd, qq):
        return remote(src, block(dd, qq), x_send.at[kind, dd, qq], x_recv.at[dd, qq], targets[kind])

    def push(src, kinds, dd, qq):
        for kind in kinds:
            hop(src, kind, dd, qq).start()

    def arrive(dd, qq):
        remote(block(dd, qq), block(dd, qq), x_send.at[2, dd, qq], x_recv.at[dd, qq], other_c).wait_recv()

    own = [
        pltpu.make_async_copy(x_ref, block(d, q), own_sem.at[0]),
        pltpu.make_async_copy(w_ref.at[d], w_rows(d), own_sem.at[1]),
        pltpu.make_async_copy(k_ref.at[d], ks.at[d], own_sem.at[2]),
    ]

    def along_z(step, k):
        origin, target = z - step * k, z + step
        here = jnp.logical_and(origin >= 0, origin < zs)
        onward = jnp.logical_and(here, jnp.logical_and(target >= 0, target < zs))
        dd = 2 * lax.rem(origin + zs, zs) + y
        target = (2 * lax.rem(target + zs, zs) + y, q)
        src = x_ref if k == 0 else block(dd, q)
        copy = remote(src, block(dd, q), z_send.at[(step + 1) // 2, k], x_recv.at[dd, q], target)
        return here, onward, dd, copy

    def forward(step, k):
        here, onward, dd, copy = along_z(step, k)
        if k > 0:
            pl.when(here)(lambda: arrive(dd, q))
        pl.when(onward)(lambda: copy.start())
        if k > 0:
            pl.when(here)(lambda: push(block(dd, q), (0, 1, 2), dd, q))

    for step in (1, -1):
        forward(step, 0)
    push(x_ref, (0, 1, 2), d, q)
    for copy in own:
        copy.start()
    moves = []
    for k, (dd, qq) in enumerate(dp_peers(n, d, q)):
        moves.append(remote(w_ref.at[dd], w_rows(d), w_send.at[k], w_recv.at[d], (dd, qq)))
        moves.append(remote(k_ref.at[dd], ks.at[d], k_send.at[k], k_recv.at[d], (dd, qq)))
    for k in range(1, zs):
        for step in (1, -1):
            forward(step, k)
        if k == 1:
            for copy in moves:
                copy.start()
    for k in range(zs):
        dd = 2 * lax.rem(z + zs - k, zs) + 1 - y
        arrive(dd, q)
        push(block(dd, q), (1, 2), dd, q)
    y_order = [2 * lax.rem(z + zs - k, zs) + (y if side == 0 else 1 - y) for side in (0, 1) for k in range(zs)]
    for dd in y_order:
        arrive(dd, other_x[1])
        push(block(dd, other_x[1]), (2,), dd, other_x[1])
    for qq in (other_c[1], 2 * (1 - x) + 1 - c):
        for dd in y_order:
            arrive(dd, qq)
    for dd, _ in dp_peers(n, d, q):
        remote(w_rows(dd), w_rows(dd), w_send.at[0], w_recv.at[dd], other_c).wait_recv()
        remote(ks.at[dd], ks.at[dd], k_send.at[0], k_recv.at[dd], other_c).wait_recv()
    for copy in moves:
        copy.wait_send()
    for dd in y_order:
        hop(block(dd, q), 1, dd, q).wait_send()
        for qq in (q, other_x[1]):
            hop(block(dd, qq), 2, dd, qq).wait_send()
    for dd in y_order[:zs]:
        hop(block(dd, q), 0, dd, q).wait_send()
    for k in range(zs):
        for step in (1, -1):
            _, onward, _, copy = along_z(step, k)
            pl.when(onward)(lambda copy=copy: copy.wait_send())
    for copy in own:
        copy.wait()


def spread(n, m, x, w, k):
    anywhere = pl.BlockSpec(memory_space=pl.ANY)
    return pl.pallas_call(
        functools.partial(spread_kernel, n),
        out_shape=(
            jax.ShapeDtypeStruct((n * x.shape[0], m * x.shape[1]), x.dtype),
            jax.ShapeDtypeStruct((n * w.shape[1], w.shape[2]), w.dtype),
            jax.ShapeDtypeStruct(k.shape, k.dtype),
        ),
        in_specs=[anywhere] * 3,
        out_specs=(anywhere,) * 3,
        scratch_shapes=[
            pltpu.SemaphoreType.DMA((2, n // 2)),
            pltpu.SemaphoreType.DMA((3, n, m)),
            pltpu.SemaphoreType.DMA((n, m)),
            pltpu.SemaphoreType.DMA((n - 1,)),
            pltpu.SemaphoreType.DMA((n,)),
            pltpu.SemaphoreType.DMA((n - 1,)),
            pltpu.SemaphoreType.DMA((n,)),
            pltpu.SemaphoreType.DMA((3,)),
        ],
        compiler_params=pltpu.CompilerParams(collective_id=0, has_side_effects=True),
        name="spread",
    )(x, w, k)


def total_kernel(n, m, part_ref, sum_ref, dp_slots, mp_slots, dp_send, dp_recv, mp_send, mp_recv):
    d, q = lax.axis_index("dp"), lax.axis_index("mp")
    over_dp, over_mp = dp_peers(n, d, q), mp_peers(m, d, q)
    greet(over_dp + over_mp)
    sum_over(d, over_dp, part_ref, part_ref, dp_slots, dp_send, dp_recv)
    column = functools.reduce(lambda a, b: a + b, [dp_slots[i] for i in range(n)])
    mp_slots[q] = column
    sends = [remote(mp_slots.at[q], mp_slots.at[q], mp_send.at[k], mp_recv.at[q], t) for k, t in enumerate(over_mp)]
    for copy in sends:
        copy.start()
    for _, qq in over_mp:
        remote(mp_slots.at[qq], mp_slots.at[qq], mp_send.at[0], mp_recv.at[qq], over_mp[0]).wait_recv()
    for copy in sends:
        copy.wait_send()
    sum_ref[...] = functools.reduce(lambda a, b: a + b, [mp_slots[i] for i in range(m)])


def sum_over(d, peers, part_ref, own_ref, slots, send, recv):
    slots[d] = own_ref[...]
    sends = [remote(part_ref, slots.at[d], send.at[k], recv.at[d], t) for k, t in enumerate(peers)]
    for copy in sends:
        copy.start()
    for dd, _ in peers:
        remote(slots.at[dd], slots.at[dd], send.at[0], recv.at[dd], peers[0]).wait_recv()
    for copy in sends:
        copy.wait_send()


def total_sum(n, m, part):
    return pl.pallas_call(
        functools.partial(total_kernel, n, m),
        out_shape=jax.ShapeDtypeStruct(part.shape, part.dtype),
        in_specs=[pl.BlockSpec(memory_space=pltpu.VMEM)],
        out_specs=pl.BlockSpec(memory_space=pltpu.VMEM),
        scratch_shapes=[
            pltpu.VMEM((n,) + part.shape, part.dtype),
            pltpu.VMEM((m,) + part.shape, part.dtype),
            pltpu.SemaphoreType.DMA((n - 1,)),
            pltpu.SemaphoreType.DMA((n,)),
            pltpu.SemaphoreType.DMA((m - 1,)),
            pltpu.SemaphoreType.DMA((m,)),
        ],
        compiler_params=pltpu.CompilerParams(collective_id=1, has_side_effects=True),
        name="total_sum",
    )(part)


def collect_kernel(
    n, m, g_ref, part_ref, gs, gain_ref, dp_slots, sums, mp_slots,
    g_send, g_recv, dp_send, dp_recv, mp_send, mp_recv, own_sem,
):
    d, q = lax.axis_index("dp"), lax.axis_index("mp")
    over_dp, over_mp = dp_peers(n, d, q), mp_peers(m, d, q)
    greet(over_dp + over_mp)
    moves = [remote(g_ref.at[t[0]], gs.at[d], g_send.at[k], g_recv.at[d], t) for k, t in enumerate(over_dp)]
    own = pltpu.make_async_copy(g_ref.at[d], gs.at[d], own_sem)
    for copy in moves:
        copy.start()
    own.start()
    sum_over(d, over_dp, part_ref, part_ref, dp_slots, dp_send, dp_recv)
    sums[...] = functools.reduce(lambda a, b: a + b, [dp_slots[i] for i in range(n)])
    mp_slots[q] = sums[q]
    sends = [remote(sums.at[t[1]], mp_slots.at[q], mp_send.at[k], mp_recv.at[q], t) for k, t in enumerate(over_mp)]
    for copy in sends:
        copy.start()
    for _, qq in over_mp:
        remote(mp_slots.at[qq], mp_slots.at[qq], mp_send.at[0], mp_recv.at[qq], over_mp[0]).wait_recv()
    for copy in sends:
        copy.wait_send()
    gain_ref[...] = functools.reduce(lambda a, b: a + b, [mp_slots[i] for i in range(m)])
    for dd, _ in over_dp:
        remote(gs.at[dd], gs.at[dd], g_send.at[0], g_recv.at[dd], over_dp[0]).wait_recv()
    for copy in moves:
        copy.wait_send()
    own.wait()


def collect(n, m, g, part):
    anywhere = pl.BlockSpec(memory_space=pl.ANY)
    inside = pl.BlockSpec(memory_space=pltpu.VMEM)
    return pl.pallas_call(
        functools.partial(collect_kernel, n, m),
        out_shape=(
            jax.ShapeDtypeStruct(g.shape, g.dtype),
            jax.ShapeDtypeStruct(part.shape[1:], part.dtype),
        ),
        in_specs=[anywhere, inside],
        out_specs=(anywhere, inside),
        scratch_shapes=[
            pltpu.VMEM((n,) + part.shape, part.dtype),
            pltpu.VMEM(part.shape, part.dtype),
            pltpu.VMEM(part.shape, part.dtype),
            pltpu.SemaphoreType.DMA((n - 1,)),
            pltpu.SemaphoreType.DMA((n,)),
            pltpu.SemaphoreType.DMA((n - 1,)),
            pltpu.SemaphoreType.DMA((n,)),
            pltpu.SemaphoreType.DMA((m - 1,)),
            pltpu.SemaphoreType.DMA((m,)),
            pltpu.SemaphoreType.DMA,
        ],
        compiler_params=pltpu.CompilerParams(collective_id=2, has_side_effects=True),
        name="collect",
    )(g, part)


def swap_halves(tile):
    return pltpu.roll(tile, LANES // 2, 1)


def by_owner_kernel(a_ref, b_ref, out_ref):
    left = lax.broadcasted_iota(jnp.int32, (a_ref.shape[0], LANES), 1) < LANES // 2
    for p in range(out_ref.shape[0] // 2):
        first, middle, last = (pl.ds((3 * p + i) * LANES, LANES) for i in range(3))
        a_mid = a_ref[:, middle].astype(jnp.float32)
        b_mid = b_ref[:, middle].astype(jnp.float32)
        out_ref[2 * p, :, :LANES] = a_ref[:, first]
        out_ref[2 * p, :, LANES : 2 * LANES] = jnp.where(left, a_mid, swap_halves(b_mid)).astype(out_ref.dtype)
        out_ref[2 * p, :, 2 * LANES :] = b_ref[:, first]
        out_ref[2 * p + 1, :, :LANES] = a_ref[:, last]
        out_ref[2 * p + 1, :, LANES : 2 * LANES] = jnp.where(left, swap_halves(a_mid), b_mid).astype(out_ref.dtype)
        out_ref[2 * p + 1, :, 2 * LANES :] = b_ref[:, last]


def by_owner(n, a, b, rows, b_from=0):
    step = min(rows, 128)
    width = a.shape[1]
    return pl.pallas_call(
        by_owner_kernel,
        grid=(rows // step,),
        out_shape=jax.ShapeDtypeStruct((n, rows, 3 * LANES), a.dtype),
        in_specs=[
            pl.BlockSpec((step, width), lambda i: (i, 0)),
            pl.BlockSpec((step, width), lambda i: (i + b_from // step, 0)),
        ],
        out_specs=pl.BlockSpec((n, step, 3 * LANES), lambda i: (0, i, 0)),
        compiler_params=pltpu.CompilerParams(vmem_limit_bytes=24 * 2**20),
        name="by_owner",
    )(a, b)


def in_place_kernel(g_ref, gate_ref, up_ref):
    left = lax.broadcasted_iota(jnp.int32, (g_ref.shape[1], LANES), 1) < LANES // 2
    for p in range(g_ref.shape[0] // 2):
        first, middle, last = (pl.ds((3 * p + i) * LANES, LANES) for i in range(3))
        one = g_ref[2 * p].astype(jnp.float32)
        two = g_ref[2 * p + 1].astype(jnp.float32)
        one_mid, two_mid = one[:, LANES : 2 * LANES], two[:, LANES : 2 * LANES]
        gate_ref[:, first] = one[:, :LANES]
        gate_ref[:, middle] = jnp.where(left, one_mid, swap_halves(two_mid))
        gate_ref[:, last] = two[:, :LANES]
        up_ref[:, first] = one[:, 2 * LANES :]
        up_ref[:, middle] = jnp.where(left, swap_halves(one_mid), two_mid)
        up_ref[:, last] = two[:, 2 * LANES :]


def in_place(g, width):
    n, rows, share = g.shape
    step = 64
    whole = pl.BlockSpec((step, width), lambda i: (i, 0))
    return pl.pallas_call(
        in_place_kernel,
        grid=(rows // step,),
        out_shape=(jax.ShapeDtypeStruct((rows, width), jnp.float32),) * 2,
        in_specs=[pl.BlockSpec((n, step, share), lambda i: (0, i, 0))],
        out_specs=(whole, whole),
        compiler_params=pltpu.CompilerParams(vmem_limit_bytes=24 * 2**20),
        name="in_place",
    )(g)


def column_pass(normed, both, upstream):
    cols = both.shape[1] // 2
    pre = jnp.dot(normed, both, preferred_element_type=jnp.float32)
    pre_up = jnp.concatenate([pre[:, 2 * LANES :], pre[:, cols : 2 * LANES]], axis=1)
    activated, back_fn = jax.vjp(activation, pre[:, :cols])
    d_up = (upstream * activated).astype(jnp.bfloat16)
    d_gate = back_fn(upstream * pre_up)[0].astype(jnp.bfloat16)
    stacked = jnp.concatenate([d_gate, d_up[:, LANES:], d_up[:, :LANES]], axis=1)
    return lax.dot_general(normed, stacked, (((0,), (0,)), ((), ())), preferred_element_type=jnp.float32)


def column_body(tokens, norm_gain, w_gate, w_up, cotangent, decay_mask, radius):
    n, m = lax.axis_size("dp"), lax.axis_size("mp")
    rows, feats = tokens.shape
    depth, width = w_gate.shape
    cols = width // n
    values = tokens.astype(jnp.float32)
    row_total = lax.psum(jnp.sum(values * values, axis=1), "mp")
    scaled = values * lax.rsqrt(row_total / (feats * m) + 1e-06)[:, None]
    normed_part = (scaled * norm_gain[None, :]).astype(jnp.bfloat16)

    w_blocks = by_owner(n, w_gate, w_up, depth)
    cot_blocks = by_owner(n, cotangent, cotangent, rows // 2, rows // 2)
    normed, both, cot = spread(n, m, normed_part, w_blocks, cot_blocks)
    whole_tile = jnp.concatenate([cot[:, :, :LANES], cot[:, :, 2 * LANES :]], axis=1)
    half_tile = jnp.concatenate([cot[:, :, LANES:cols], cot[:, :, cols : 2 * LANES]], axis=1)
    upstream = jnp.concatenate([whole_tile, half_tile], axis=2)
    upstream = upstream.reshape(n * rows, cols).astype(jnp.float32)

    groups = decay_mask.astype(jnp.float32)
    is_gate = lax.broadcasted_iota(jnp.int32, (1, 2 * cols), 1) < cols
    mask = jnp.where(is_gate, groups[0][:, None], groups[1][:, None])
    asc = column_pass(normed, both, upstream).astype(jnp.bfloat16).astype(jnp.float32)
    part = jnp.sum(mask * asc * asc)
    total = total_sum(n, m, jnp.full((8, 128), part, jnp.float32))[0, 0]
    factor = radius[0] / (jnp.sqrt(total) + 1e-12)
    moved = (both.astype(jnp.float32) + factor * mask * asc).astype(jnp.bfloat16)

    grads = column_pass(normed, moved, upstream)
    gain_part = jnp.sum(moved.astype(jnp.float32) * grads, axis=1)
    grads = grads.astype(jnp.bfloat16).reshape(n, depth, 2 * cols)
    grads, gain_sum = collect(n, m, grads, gain_part.reshape(m, 8, feats // 8))
    d_gain = gain_sum.reshape(feats) / norm_gain
    return (d_gain,) + tuple(in_place(grads, width))


def activation(value):
    return jax.nn.gelu(value, approximate=True)


def fetch_weights(part_gate, part_up):
    return (
        lax.all_gather(part_gate, "dp", axis=0, tiled=True),
        lax.all_gather(part_up, "dp", axis=0, tiled=True),
    )


def one_pass(scaled_rows, gain_part, full_gate, full_up, cotangent):
    hidden_width = full_gate.shape[1]
    normed_part = (scaled_rows * gain_part[None, :]).astype(jnp.bfloat16)
    normed = lax.all_gather(normed_part, "mp", axis=1, tiled=True)
    pre_gate = jnp.dot(normed, full_gate, preferred_element_type=jnp.float32)
    pre_up = jnp.dot(normed, full_up, preferred_element_type=jnp.float32)
    activated, back_fn = jax.vjp(activation, pre_gate)
    upstream = cotangent.astype(jnp.float32)
    d_up = (upstream * activated).astype(jnp.bfloat16)
    d_gate = back_fn(upstream * pre_up)[0].astype(jnp.bfloat16)
    feature_term = lax.dot_general(
        d_gate, full_gate, (((1,), (1,)), ((), ())), preferred_element_type=jnp.float32
    )
    feature_term = feature_term + lax.dot_general(
        d_up, full_up, (((1,), (1,)), ((), ())), preferred_element_type=jnp.float32
    )
    d_norm = lax.psum_scatter(
        feature_term.astype(jnp.bfloat16), "mp", scatter_dimension=1, tiled=True
    ).astype(jnp.float32)
    d_gain = lax.psum(jnp.sum(d_norm * scaled_rows, axis=0), "dp")
    stacked = jnp.concatenate([d_gate, d_up], axis=1)
    both = lax.psum_scatter(
        lax.dot_general(
            normed, stacked, (((0,), (0,)), ((), ())), preferred_element_type=jnp.float32
        ).astype(jnp.bfloat16),
        "dp",
        scatter_dimension=0,
        tiled=True,
    ).astype(jnp.float32)
    return (d_gain, both[:, :hidden_width], both[:, hidden_width:])


def body(tokens, norm_gain, w_gate, w_up, cotangent, decay_mask, radius):
    values = tokens.astype(jnp.float32)
    width = values.shape[1] * lax.axis_size("mp")
    row_total = lax.psum(jnp.sum(values * values, axis=1), "mp")
    scaled_rows = values * lax.rsqrt(row_total / width + 1e-06)[:, None]
    groups = decay_mask.astype(jnp.float32)
    local_rows = w_gate.shape[0]
    first_row = lax.axis_index("dp") * local_rows
    local_groups = lax.dynamic_slice_in_dim(groups, first_row, local_rows, 1)
    gate_mask = local_groups[0][:, None]
    up_mask = local_groups[1][:, None]
    full_gate, full_up = fetch_weights(w_gate, w_up)
    asc_gain, asc_gate_f, asc_up_f = one_pass(scaled_rows, norm_gain, full_gate, full_up, cotangent)
    gate_low = asc_gate_f.astype(jnp.bfloat16)
    up_low = asc_up_f.astype(jnp.bfloat16)
    gate_wide = gate_low.astype(jnp.float32)
    up_wide = up_low.astype(jnp.float32)
    matrix_part = jnp.sum(gate_mask * gate_wide * gate_wide) + jnp.sum(up_mask * up_wide * up_wide)
    total = lax.psum(matrix_part, ("dp", "mp"))
    factor = radius[0] / (jnp.sqrt(total) + 1e-12)
    new_gate = (w_gate.astype(jnp.float32) + factor * gate_mask * gate_wide).astype(jnp.bfloat16)
    new_up = (w_up.astype(jnp.float32) + factor * up_mask * up_wide).astype(jnp.bfloat16)
    next_gate, next_up = fetch_weights(new_gate, new_up)
    return one_pass(scaled_rows, norm_gain, next_gate, next_up, cotangent)


def either_body(tokens, norm_gain, w_gate, *rest):
    n, m = lax.axis_size("dp"), lax.axis_size("mp")
    by_columns = m == 4 and n % 2 == 0 and 2 * w_gate.shape[1] == 3 * LANES * n
    return (column_body if by_columns else body)(tokens, norm_gain, w_gate, *rest)


def solution(mesh):
    placed = (P("dp", "mp"), P("mp"), P("dp", "mp"), P("dp", "mp"), P("dp", "mp"), P(), P())
    return jax.shard_map(
        either_body,
        mesh=mesh,
        in_specs=placed,
        out_specs=(P("mp"), P("dp", "mp"), P("dp", "mp")),
        check_vma=False,
    )
```

```python
import functools

import jax
import jax.numpy as jnp
from jax import lax
from jax.experimental import pallas as pl
from jax.experimental.pallas import tpu as pltpu
from jax.sharding import PartitionSpec as P

MESH = pl.DeviceIdType.MESH
LANES = 128


def remote(src, dst, send_sem, recv_sem, target):
    return pltpu.make_async_remote_copy(
        src_ref=src,
        dst_ref=dst,
        send_sem=send_sem,
        recv_sem=recv_sem,
        device_id=target,
        device_id_type=MESH,
    )


def greet(targets):
    barrier = pltpu.get_barrier_semaphore()
    for target in targets:
        pl.semaphore_signal(barrier, inc=1, device_id=target, device_id_type=MESH)
    pl.semaphore_wait(barrier, len(targets))


def dp_peers(n, d, q):
    return [(lax.rem(d + k, n), q) for k in range(1, n)]


def mp_peers(m, d, q):
    return [(d, lax.rem(q + k, m)) for k in range(1, m)]


def spread_kernel(
    n, x_ref, w_ref, k_ref, xs, ws, ks, z_send, x_send, x_recv, w_send, w_recv, k_send, k_recv, own_sem
):
    d, q = lax.axis_index("dp"), lax.axis_index("mp")
    rows, feats = x_ref.shape
    depth = w_ref.shape[1]
    zs = n // 2
    z, y = d // 2, lax.rem(d, 2)
    x, c = q // 2, lax.rem(q, 2)
    other_y, other_x, other_c = (2 * z + 1 - y, q), (d, 2 * (1 - x) + c), (d, 2 * x + 1 - c)
    greet(dp_peers(n, d, q) + [other_x, other_c])

    def block(dd, qq):
        return xs.at[
            pl.ds(pl.multiple_of(dd * rows, rows), rows), pl.ds(pl.multiple_of(qq * feats, feats), feats)
        ]

    def w_rows(dd):
        return ws.at[pl.ds(pl.multiple_of(dd * depth, depth), depth)]

    targets = (other_y, other_x, other_c)

    def hop(src, kind, dd, qq):
        return remote(src, block(dd, qq), x_send.at[kind, dd, qq], x_recv.at[dd, qq], targets[kind])

    def push(src, kinds, dd, qq):
        for kind in kinds:
            hop(src, kind, dd, qq).start()

    def arrive(dd, qq):
        remote(block(dd, qq), block(dd, qq), x_send.at[2, dd, qq], x_recv.at[dd, qq], other_c).wait_recv()

    own = [
        pltpu.make_async_copy(x_ref, block(d, q), own_sem.at[0]),
        pltpu.make_async_copy(w_ref.at[d], w_rows(d), own_sem.at[1]),
        pltpu.make_async_copy(k_ref.at[d], ks.at[d], own_sem.at[2]),
    ]

    def along_z(step, k):
        origin, target = z - step * k, z + step
        here = jnp.logical_and(origin >= 0, origin < zs)
        onward = jnp.logical_and(here, jnp.logical_and(target >= 0, target < zs))
        dd = 2 * lax.rem(origin + zs, zs) + y
        target = (2 * lax.rem(target + zs, zs) + y, q)
        src = x_ref if k == 0 else block(dd, q)
        copy = remote(src, block(dd, q), z_send.at[(step + 1) // 2, k], x_recv.at[dd, q], target)
        return here, onward, dd, copy

    def forward(step, k):
        here, onward, dd, copy = along_z(step, k)
        if k > 0:
            pl.when(here)(lambda: arrive(dd, q))
        pl.when(onward)(lambda: copy.start())
        if k > 0:
            pl.when(here)(lambda: push(block(dd, q), (0, 1, 2), dd, q))

    for step in (1, -1):
        forward(step, 0)
    push(x_ref, (0, 1, 2), d, q)
    for copy in own:
        copy.start()
    moves = []
    for k, (dd, qq) in enumerate(dp_peers(n, d, q)):
        moves.append(remote(w_ref.at[dd], w_rows(d), w_send.at[k], w_recv.at[d], (dd, qq)))
        moves.append(remote(k_ref.at[dd], ks.at[d], k_send.at[k], k_recv.at[d], (dd, qq)))
    for k in range(1, zs):
        for step in (1, -1):
            forward(step, k)
        if k == zs - 2:
            for copy in moves:
                copy.start()
    for k in range(zs):
        dd = 2 * lax.rem(z + zs - k, zs) + 1 - y
        arrive(dd, q)
        push(block(dd, q), (1, 2), dd, q)
    y_order = [2 * lax.rem(z + zs - k, zs) + (y if side == 0 else 1 - y) for side in (0, 1) for k in range(zs)]
    for dd in y_order:
        arrive(dd, other_x[1])
        push(block(dd, other_x[1]), (2,), dd, other_x[1])
    for qq in (other_c[1], 2 * (1 - x) + 1 - c):
        for dd in y_order:
            arrive(dd, qq)
    for dd, _ in dp_peers(n, d, q):
        remote(w_rows(dd), w_rows(dd), w_send.at[0], w_recv.at[dd], other_c).wait_recv()
        remote(ks.at[dd], ks.at[dd], k_send.at[0], k_recv.at[dd], other_c).wait_recv()
    for copy in moves:
        copy.wait_send()
    for dd in y_order:
        hop(block(dd, q), 1, dd, q).wait_send()
        for qq in (q, other_x[1]):
            hop(block(dd, qq), 2, dd, qq).wait_send()
    for dd in y_order[:zs]:
        hop(block(dd, q), 0, dd, q).wait_send()
    for k in range(zs):
        for step in (1, -1):
            _, onward, _, copy = along_z(step, k)
            pl.when(onward)(lambda copy=copy: copy.wait_send())
    for copy in own:
        copy.wait()


def spread(n, m, x, w, k):
    anywhere = pl.BlockSpec(memory_space=pl.ANY)
    return pl.pallas_call(
        functools.partial(spread_kernel, n),
        out_shape=(
            jax.ShapeDtypeStruct((n * x.shape[0], m * x.shape[1]), x.dtype),
            jax.ShapeDtypeStruct((n * w.shape[1], w.shape[2]), w.dtype),
            jax.ShapeDtypeStruct(k.shape, k.dtype),
        ),
        in_specs=[anywhere] * 3,
        out_specs=(anywhere,) * 3,
        scratch_shapes=[
            pltpu.SemaphoreType.DMA((2, n // 2)),
            pltpu.SemaphoreType.DMA((3, n, m)),
            pltpu.SemaphoreType.DMA((n, m)),
            pltpu.SemaphoreType.DMA((n - 1,)),
            pltpu.SemaphoreType.DMA((n,)),
            pltpu.SemaphoreType.DMA((n - 1,)),
            pltpu.SemaphoreType.DMA((n,)),
            pltpu.SemaphoreType.DMA((3,)),
        ],
        compiler_params=pltpu.CompilerParams(collective_id=0, has_side_effects=True),
        name="spread",
    )(x, w, k)


def total_kernel(n, m, part_ref, sum_ref, dp_slots, mp_slots, dp_send, dp_recv, mp_send, mp_recv):
    d, q = lax.axis_index("dp"), lax.axis_index("mp")
    over_dp, over_mp = dp_peers(n, d, q), mp_peers(m, d, q)
    greet(over_dp + over_mp)
    sum_over(d, over_dp, part_ref, part_ref, dp_slots, dp_send, dp_recv)
    column = functools.reduce(lambda a, b: a + b, [dp_slots[i] for i in range(n)])
    mp_slots[q] = column
    sends = [remote(mp_slots.at[q], mp_slots.at[q], mp_send.at[k], mp_recv.at[q], t) for k, t in enumerate(over_mp)]
    for copy in sends:
        copy.start()
    for _, qq in over_mp:
        remote(mp_slots.at[qq], mp_slots.at[qq], mp_send.at[0], mp_recv.at[qq], over_mp[0]).wait_recv()
    for copy in sends:
        copy.wait_send()
    sum_ref[...] = functools.reduce(lambda a, b: a + b, [mp_slots[i] for i in range(m)])


def sum_over(d, peers, part_ref, own_ref, slots, send, recv):
    slots[d] = own_ref[...]
    sends = [remote(part_ref, slots.at[d], send.at[k], recv.at[d], t) for k, t in enumerate(peers)]
    for copy in sends:
        copy.start()
    for dd, _ in peers:
        remote(slots.at[dd], slots.at[dd], send.at[0], recv.at[dd], peers[0]).wait_recv()
    for copy in sends:
        copy.wait_send()


def total_sum(n, m, part):
    return pl.pallas_call(
        functools.partial(total_kernel, n, m),
        out_shape=jax.ShapeDtypeStruct(part.shape, part.dtype),
        in_specs=[pl.BlockSpec(memory_space=pltpu.VMEM)],
        out_specs=pl.BlockSpec(memory_space=pltpu.VMEM),
        scratch_shapes=[
            pltpu.VMEM((n,) + part.shape, part.dtype),
            pltpu.VMEM((m,) + part.shape, part.dtype),
            pltpu.SemaphoreType.DMA((n - 1,)),
            pltpu.SemaphoreType.DMA((n,)),
            pltpu.SemaphoreType.DMA((m - 1,)),
            pltpu.SemaphoreType.DMA((m,)),
        ],
        compiler_params=pltpu.CompilerParams(collective_id=1, has_side_effects=True),
        name="total_sum",
    )(part)


def collect_kernel(
    n, m, g_ref, part_ref, gs, gain_ref, dp_slots, sums, mp_slots,
    g_send, g_recv, dp_send, dp_recv, mp_send, mp_recv, own_sem,
):
    d, q = lax.axis_index("dp"), lax.axis_index("mp")
    over_dp, over_mp = dp_peers(n, d, q), mp_peers(m, d, q)
    greet(over_dp + over_mp)
    moves = [remote(g_ref.at[t[0]], gs.at[d], g_send.at[k], g_recv.at[d], t) for k, t in enumerate(over_dp)]
    own = pltpu.make_async_copy(g_ref.at[d], gs.at[d], own_sem)
    for copy in moves:
        copy.start()
    own.start()
    sum_over(d, over_dp, part_ref, part_ref, dp_slots, dp_send, dp_recv)
    sums[...] = functools.reduce(lambda a, b: a + b, [dp_slots[i] for i in range(n)])
    mp_slots[q] = sums[q]
    sends = [remote(sums.at[t[1]], mp_slots.at[q], mp_send.at[k], mp_recv.at[q], t) for k, t in enumerate(over_mp)]
    for copy in sends:
        copy.start()
    for _, qq in over_mp:
        remote(mp_slots.at[qq], mp_slots.at[qq], mp_send.at[0], mp_recv.at[qq], over_mp[0]).wait_recv()
    for copy in sends:
        copy.wait_send()
    gain_ref[...] = functools.reduce(lambda a, b: a + b, [mp_slots[i] for i in range(m)])
    for dd, _ in over_dp:
        remote(gs.at[dd], gs.at[dd], g_send.at[0], g_recv.at[dd], over_dp[0]).wait_recv()
    for copy in moves:
        copy.wait_send()
    own.wait()


def collect(n, m, g, part):
    anywhere = pl.BlockSpec(memory_space=pl.ANY)
    inside = pl.BlockSpec(memory_space=pltpu.VMEM)
    return pl.pallas_call(
        functools.partial(collect_kernel, n, m),
        out_shape=(
            jax.ShapeDtypeStruct(g.shape, g.dtype),
            jax.ShapeDtypeStruct(part.shape[1:], part.dtype),
        ),
        in_specs=[anywhere, inside],
        out_specs=(anywhere, inside),
        scratch_shapes=[
            pltpu.VMEM((n,) + part.shape, part.dtype),
            pltpu.VMEM(part.shape, part.dtype),
            pltpu.VMEM(part.shape, part.dtype),
            pltpu.SemaphoreType.DMA((n - 1,)),
            pltpu.SemaphoreType.DMA((n,)),
            pltpu.SemaphoreType.DMA((n - 1,)),
            pltpu.SemaphoreType.DMA((n,)),
            pltpu.SemaphoreType.DMA((m - 1,)),
            pltpu.SemaphoreType.DMA((m,)),
            pltpu.SemaphoreType.DMA,
        ],
        compiler_params=pltpu.CompilerParams(collective_id=2, has_side_effects=True),
        name="collect",
    )(g, part)


def swap_halves(tile):
    return pltpu.roll(tile, LANES // 2, 1)


def by_owner_kernel(a_ref, b_ref, out_ref):
    left = lax.broadcasted_iota(jnp.int32, (a_ref.shape[0], LANES), 1) < LANES // 2
    for p in range(out_ref.shape[0] // 2):
        first, middle, last = (pl.ds((3 * p + i) * LANES, LANES) for i in range(3))
        a_mid = a_ref[:, middle].astype(jnp.float32)
        b_mid = b_ref[:, middle].astype(jnp.float32)
        out_ref[2 * p, :, :LANES] = a_ref[:, first]
        out_ref[2 * p, :, LANES : 2 * LANES] = jnp.where(left, a_mid, swap_halves(b_mid)).astype(out_ref.dtype)
        out_ref[2 * p, :, 2 * LANES :] = b_ref[:, first]
        out_ref[2 * p + 1, :, :LANES] = a_ref[:, last]
        out_ref[2 * p + 1, :, LANES : 2 * LANES] = jnp.where(left, swap_halves(a_mid), b_mid).astype(out_ref.dtype)
        out_ref[2 * p + 1, :, 2 * LANES :] = b_ref[:, last]


def by_owner(n, a, b, rows, b_from=0):
    step = min(rows, 128)
    width = a.shape[1]
    return pl.pallas_call(
        by_owner_kernel,
        grid=(rows // step,),
        out_shape=jax.ShapeDtypeStruct((n, rows, 3 * LANES), a.dtype),
        in_specs=[
            pl.BlockSpec((step, width), lambda i: (i, 0)),
            pl.BlockSpec((step, width), lambda i: (i + b_from // step, 0)),
        ],
        out_specs=pl.BlockSpec((n, step, 3 * LANES), lambda i: (0, i, 0)),
        compiler_params=pltpu.CompilerParams(vmem_limit_bytes=24 * 2**20),
        name="by_owner",
    )(a, b)


def in_place_kernel(g_ref, gate_ref, up_ref):
    left = lax.broadcasted_iota(jnp.int32, (g_ref.shape[1], LANES), 1) < LANES // 2
    for p in range(g_ref.shape[0] // 2):
        first, middle, last = (pl.ds((3 * p + i) * LANES, LANES) for i in range(3))
        one = g_ref[2 * p].astype(jnp.float32)
        two = g_ref[2 * p + 1].astype(jnp.float32)
        one_mid, two_mid = one[:, LANES : 2 * LANES], two[:, LANES : 2 * LANES]
        gate_ref[:, first] = one[:, :LANES]
        gate_ref[:, middle] = jnp.where(left, one_mid, swap_halves(two_mid))
        gate_ref[:, last] = two[:, :LANES]
        up_ref[:, first] = one[:, 2 * LANES :]
        up_ref[:, middle] = jnp.where(left, swap_halves(one_mid), two_mid)
        up_ref[:, last] = two[:, 2 * LANES :]


def in_place(g, width):
    n, rows, share = g.shape
    step = 64
    whole = pl.BlockSpec((step, width), lambda i: (i, 0))
    return pl.pallas_call(
        in_place_kernel,
        grid=(rows // step,),
        out_shape=(jax.ShapeDtypeStruct((rows, width), jnp.float32),) * 2,
        in_specs=[pl.BlockSpec((n, step, share), lambda i: (0, i, 0))],
        out_specs=(whole, whole),
        compiler_params=pltpu.CompilerParams(vmem_limit_bytes=24 * 2**20),
        name="in_place",
    )(g)


def column_pass(normed, both, upstream):
    cols = both.shape[1] // 2
    pre = jnp.dot(normed, both, preferred_element_type=jnp.float32)
    pre_up = jnp.concatenate([pre[:, 2 * LANES :], pre[:, cols : 2 * LANES]], axis=1)
    activated, back_fn = jax.vjp(activation, pre[:, :cols])
    d_up = (upstream * activated).astype(jnp.bfloat16)
    d_gate = back_fn(upstream * pre_up)[0].astype(jnp.bfloat16)
    stacked = jnp.concatenate([d_gate, d_up[:, LANES:], d_up[:, :LANES]], axis=1)
    return lax.dot_general(normed, stacked, (((0,), (0,)), ((), ())), preferred_element_type=jnp.float32)


def column_body(tokens, norm_gain, w_gate, w_up, cotangent, decay_mask, radius):
    n, m = lax.axis_size("dp"), lax.axis_size("mp")
    rows, feats = tokens.shape
    depth, width = w_gate.shape
    cols = width // n
    values = tokens.astype(jnp.float32)
    row_total = lax.psum(jnp.sum(values * values, axis=1), "mp")
    scaled = values * lax.rsqrt(row_total / (feats * m) + 1e-06)[:, None]
    normed_part = (scaled * norm_gain[None, :]).astype(jnp.bfloat16)

    w_blocks = by_owner(n, w_gate, w_up, depth)
    cot_blocks = by_owner(n, cotangent, cotangent, rows // 2, rows // 2)
    normed, both, cot = spread(n, m, normed_part, w_blocks, cot_blocks)
    whole_tile = jnp.concatenate([cot[:, :, :LANES], cot[:, :, 2 * LANES :]], axis=1)
    half_tile = jnp.concatenate([cot[:, :, LANES:cols], cot[:, :, cols : 2 * LANES]], axis=1)
    upstream = jnp.concatenate([whole_tile, half_tile], axis=2)
    upstream = upstream.reshape(n * rows, cols).astype(jnp.float32)

    groups = decay_mask.astype(jnp.float32)
    is_gate = lax.broadcasted_iota(jnp.int32, (1, 2 * cols), 1) < cols
    mask = jnp.where(is_gate, groups[0][:, None], groups[1][:, None])
    asc = column_pass(normed, both, upstream).astype(jnp.bfloat16).astype(jnp.float32)
    part = jnp.sum(mask * asc * asc)
    total = total_sum(n, m, jnp.full((8, 128), part, jnp.float32))[0, 0]
    factor = radius[0] / (jnp.sqrt(total) + 1e-12)
    moved = (both.astype(jnp.float32) + factor * mask * asc).astype(jnp.bfloat16)

    grads = column_pass(normed, moved, upstream)
    gain_part = jnp.sum(moved.astype(jnp.float32) * grads, axis=1)
    grads = grads.astype(jnp.bfloat16).reshape(n, depth, 2 * cols)
    grads, gain_sum = collect(n, m, grads, gain_part.reshape(m, 8, feats // 8))
    d_gain = gain_sum.reshape(feats) / norm_gain
    return (d_gain,) + tuple(in_place(grads, width))


def activation(value):
    return jax.nn.gelu(value, approximate=True)


def fetch_weights(part_gate, part_up):
    return (
        lax.all_gather(part_gate, "dp", axis=0, tiled=True),
        lax.all_gather(part_up, "dp", axis=0, tiled=True),
    )


def one_pass(scaled_rows, gain_part, full_gate, full_up, cotangent):
    hidden_width = full_gate.shape[1]
    normed_part = (scaled_rows * gain_part[None, :]).astype(jnp.bfloat16)
    normed = lax.all_gather(normed_part, "mp", axis=1, tiled=True)
    pre_gate = jnp.dot(normed, full_gate, preferred_element_type=jnp.float32)
    pre_up = jnp.dot(normed, full_up, preferred_element_type=jnp.float32)
    activated, back_fn = jax.vjp(activation, pre_gate)
    upstream = cotangent.astype(jnp.float32)
    d_up = (upstream * activated).astype(jnp.bfloat16)
    d_gate = back_fn(upstream * pre_up)[0].astype(jnp.bfloat16)
    feature_term = lax.dot_general(
        d_gate, full_gate, (((1,), (1,)), ((), ())), preferred_element_type=jnp.float32
    )
    feature_term = feature_term + lax.dot_general(
        d_up, full_up, (((1,), (1,)), ((), ())), preferred_element_type=jnp.float32
    )
    d_norm = lax.psum_scatter(
        feature_term.astype(jnp.bfloat16), "mp", scatter_dimension=1, tiled=True
    ).astype(jnp.float32)
    d_gain = lax.psum(jnp.sum(d_norm * scaled_rows, axis=0), "dp")
    stacked = jnp.concatenate([d_gate, d_up], axis=1)
    both = lax.psum_scatter(
        lax.dot_general(
            normed, stacked, (((0,), (0,)), ((), ())), preferred_element_type=jnp.float32
        ).astype(jnp.bfloat16),
        "dp",
        scatter_dimension=0,
        tiled=True,
    ).astype(jnp.float32)
    return (d_gain, both[:, :hidden_width], both[:, hidden_width:])


def body(tokens, norm_gain, w_gate, w_up, cotangent, decay_mask, radius):
    values = tokens.astype(jnp.float32)
    width = values.shape[1] * lax.axis_size("mp")
    row_total = lax.psum(jnp.sum(values * values, axis=1), "mp")
    scaled_rows = values * lax.rsqrt(row_total / width + 1e-06)[:, None]
    groups = decay_mask.astype(jnp.float32)
    local_rows = w_gate.shape[0]
    first_row = lax.axis_index("dp") * local_rows
    local_groups = lax.dynamic_slice_in_dim(groups, first_row, local_rows, 1)
    gate_mask = local_groups[0][:, None]
    up_mask = local_groups[1][:, None]
    full_gate, full_up = fetch_weights(w_gate, w_up)
    asc_gain, asc_gate_f, asc_up_f = one_pass(scaled_rows, norm_gain, full_gate, full_up, cotangent)
    gate_low = asc_gate_f.astype(jnp.bfloat16)
    up_low = asc_up_f.astype(jnp.bfloat16)
    gate_wide = gate_low.astype(jnp.float32)
    up_wide = up_low.astype(jnp.float32)
    matrix_part = jnp.sum(gate_mask * gate_wide * gate_wide) + jnp.sum(up_mask * up_wide * up_wide)
    total = lax.psum(matrix_part, ("dp", "mp"))
    factor = radius[0] / (jnp.sqrt(total) + 1e-12)
    new_gate = (w_gate.astype(jnp.float32) + factor * gate_mask * gate_wide).astype(jnp.bfloat16)
    new_up = (w_up.astype(jnp.float32) + factor * up_mask * up_wide).astype(jnp.bfloat16)
    next_gate, next_up = fetch_weights(new_gate, new_up)
    return one_pass(scaled_rows, norm_gain, next_gate, next_up, cotangent)


def either_body(tokens, norm_gain, w_gate, *rest):
    n, m = lax.axis_size("dp"), lax.axis_size("mp")
    by_columns = m == 4 and n % 2 == 0 and 2 * w_gate.shape[1] == 3 * LANES * n
    return (column_body if by_columns else body)(tokens, norm_gain, w_gate, *rest)


def solution(mesh):
    placed = (P("dp", "mp"), P("mp"), P("dp", "mp"), P("dp", "mp"), P("dp", "mp"), P(), P())
    return jax.shard_map(
        either_body,
        mesh=mesh,
        in_specs=placed,
        out_specs=(P("mp"), P("dp", "mp"), P("dp", "mp")),
        check_vma=False,
    )
```
